32 devices in a mesh: win: 2 (over y), sta: 4 (over z), seg: 2 (over x), frq: 2 (over core).
Axes of the slice: x: 2, y: 2, z: 4, core: 2. Of those that a mesh axis runs over, the one named last changes fastest.
Arguments:
- ingest: bfloat16 [4, 2048, 512], P(('win', 'seg'), 'sta'), parts along dimension 0
- seg_offsets: int32 [4], P(('win', 'seg')), parts along dimension 0, may hold values from 0 to 2047
- pair_blocks: int32 [2, 24], P(None, 'sta'), may hold values from 0 to 63, as said below
- pair_count: int32 [4], P('sta'), may hold values from 1 to 6, as said below
Outputs:
- correlations: float32 [1200, 3072], P(('seg', 'frq'), ('win', 'sta')), parts along dimension 1
The draws below stay inside these ranges and needn't reach their ends.
There are 2 independent parts, one for each index of `win`. The reference program is written for one: setup_inputs(seed, part) draws one part's arguments, and reference() takes and returns one part's arrays. A program takes and returns all parts, laid end to end along the dimension named above; an argument that names none is the same for every part. Nothing has to cross between parts.
Inputs may be any that keep to these rules, and one draw needn't show every extreme that they name: `pair_count`: each owner's number of live slots; they sum to exactly 12, and some owner has exactly 6. `pair_blocks`: column q lists the blocks of slot q, owned by q // 6; row 0 names a block that this owner holds, (q // 6) * 16 to that plus 16 - 1; row 1 names any block; of one owner's 6 slots at most 2 have their second block on any one owner, and some owner holds exactly 2 of them; the second blocks of the owners' first slots lie on distinct owners.
All inputs are finite; a program needn't handle non-finite values.
Results may differ from the reference program's by a relative error of at most 0.0054.
Values may be sent and summed in bfloat16 or wider, within the bound.
A program may use at most 64 MiB of HBM per device.

```python
import math
import jax
import jax.numpy as jnp
from jax import lax

SEG_LEN = 2048
MAXLAG = 600
BLOCK_STA = 8
BLK_DEV = 16
PAIR_CAP = 6
LIVE_DEV = 3
HOLD_CAP = 2
OWNERS = 4
STATIONS = 512
SEGMENTS = 2
PAIR_SLOTS = 24


def draw_ingest(key, part):
    key = jax.random.fold_in(key, 1)
    gain_key, noise_key = jax.random.split(key, 2)
    gains = jnp.exp(jax.random.uniform(gain_key, (1, 1, STATIONS), jnp.float32, math.log(0.2), math.log(5.0)))
    noise = jax.random.normal(noise_key, (SEGMENTS, SEG_LEN, STATIONS), jnp.float32)
    values = jnp.clip(noise, -6.0, 6.0) * gains
    return values.astype(jnp.bfloat16)


def draw_pair_blocks(key, part):
    key = jax.random.fold_in(key, 2)
    sub_keys = jax.random.split(key, 4)
    slot_number = jnp.arange(PAIR_SLOTS, dtype=jnp.int32)
    slot_owner = slot_number // PAIR_CAP
    slot_rank = slot_number % PAIR_CAP
    first_rows = slot_owner * BLK_DEV + jax.random.randint(sub_keys[0], (PAIR_SLOTS,), 0, BLK_DEV, dtype=jnp.int32)
    offset_owner = jax.random.randint(sub_keys[2], (), 1, OWNERS, dtype=jnp.int32)
    second_owner = (slot_owner + offset_owner + slot_rank // HOLD_CAP) % OWNERS
    inside = jax.random.randint(sub_keys[1], (PAIR_SLOTS,), 0, BLK_DEV, dtype=jnp.int32)
    lead_inside = jax.random.randint(sub_keys[3], (PAIR_SLOTS,), 0, BLK_DEV, dtype=jnp.int32)
    lead_inside = jnp.where(second_owner == 0, 0, jnp.where(second_owner == OWNERS - 1, BLK_DEV - 1, lead_inside))
    is_lead = slot_rank == 0
    partner = second_owner * BLK_DEV + jnp.where(is_lead, lead_inside, inside)
    return jnp.stack([first_rows, partner]).astype(jnp.int32)


def draw_pair_count(key, part):
    key = jax.random.fold_in(key, 3)
    lead_key, loop_key = jax.random.split(key, 2)
    owner_ids = jnp.arange(OWNERS, dtype=jnp.int32)
    lead_owner = jax.random.randint(lead_key, (), 0, OWNERS, dtype=jnp.int32)
    start_counts = jnp.where(owner_ids == lead_owner, PAIR_CAP, LIVE_DEV).astype(jnp.int32)
    target_total = LIVE_DEV * OWNERS

    def one_move(step_number, counts):
        step_key = jax.random.fold_in(loop_key, step_number)
        give_key, take_key = jax.random.split(step_key, 2)
        give_score = jax.random.randint(give_key, (OWNERS,), 0, 1 << 20, dtype=jnp.int32)
        take_score = jax.random.randint(take_key, (OWNERS,), 0, 1 << 20, dtype=jnp.int32)
        surplus = jnp.sum(counts) - target_total
        give_ok = (owner_ids != lead_owner) & (counts > 1)
        take_ok = (owner_ids != lead_owner) & (counts < PAIR_CAP - 1) & (surplus <= 0)
        giver = jnp.argmax(jnp.where(give_ok, give_score, -1)).astype(jnp.int32)
        taker = jnp.argmax(jnp.where(take_ok, take_score, -1)).astype(jnp.int32)
        can_take = jnp.any(take_ok) & (taker != giver)
        act = jnp.any(give_ok) & ((surplus > 0) | can_take)
        delta = jnp.where(owner_ids == giver, -1, 0) + jnp.where((owner_ids == taker) & can_take & (surplus <= 0), 1, 0)
        return (counts + jnp.where(act, delta, 0)).astype(jnp.int32)
    counts = lax.fori_loop(0, 4 * OWNERS + PAIR_CAP, one_move, start_counts)
    return counts.astype(jnp.int32)


def setup_inputs(seed: int = 0, part: int = 0) -> dict:
    key_list = jax.random.split(jax.random.key(seed), 5)
    part_keys = jax.random.split(jax.random.fold_in(key_list[4], part), 5)
    return {
        "ingest": draw_ingest(jax.random.fold_in(jax.random.fold_in(key_list[4], part), 71), part),
        "seg_offsets": jax.random.randint(part_keys[1], (SEGMENTS,), 0, SEG_LEN).astype(jnp.int32),
        "pair_blocks": draw_pair_blocks(jax.random.fold_in(key_list[4], 71), part),
        "pair_count": draw_pair_count(jax.random.fold_in(key_list[4], 71), part),
    }


HALF_TAPS = 10
NOISE_BASELINE = 0.5

def whiten(traces):
    spectral_magnitude = jnp.abs(traces.astype(jnp.float32))
    padded = jnp.pad(spectral_magnitude, ((0, 0), (HALF_TAPS, HALF_TAPS), (0, 0)))
    record_span_duration = traces.shape[1]
    levels = padded[:, 0:record_span_duration, :]
    for shift_step in range(1, 2 * HALF_TAPS + 1):
        levels = levels + padded[:, shift_step:shift_step + record_span_duration, :]
    levels = levels / (2 * HALF_TAPS + 1)
    return (traces.astype(jnp.float32) / jnp.maximum(levels, NOISE_BASELINE)).astype(jnp.bfloat16)

def dft_table(first_bin, bin_count, record_span_duration):
    oscillation_duration = 2 * record_span_duration
    fourier_mode_number = first_bin + jnp.arange(bin_count, dtype=jnp.int32)
    recording_moments = jnp.arange(record_span_duration, dtype=jnp.int32)
    rotation_increment_number = fourier_mode_number[:, None] * recording_moments[None, :] % oscillation_duration
    angles = rotation_increment_number.astype(jnp.float32) * (2.0 * math.pi / oscillation_duration)
    return jnp.concatenate([jnp.cos(angles), -jnp.sin(angles)], 0).astype(jnp.bfloat16)

def lag_offsets_table(first_lag, lag_count, first_bin, bin_count, record_span_duration, segments, max_lag):
    oscillation_duration = 2 * record_span_duration
    lag_values = first_lag + jnp.arange(lag_count, dtype=jnp.int32) - max_lag
    fourier_mode_number = first_bin + jnp.arange(bin_count, dtype=jnp.int32)
    rotation_increment_number = fourier_mode_number[None, :] * (lag_values[:, None] % oscillation_duration) % oscillation_duration
    angles = rotation_increment_number.astype(jnp.float32) * (2.0 * math.pi / oscillation_duration)
    weights = jnp.where(fourier_mode_number == 0, 1.0, 2.0).astype(jnp.float32)[None, :]
    norm_scale = 1.0 / (oscillation_duration * math.sqrt(record_span_duration * segments))
    return jnp.concatenate([jnp.cos(angles) * weights, -jnp.sin(angles) * weights], 1) * norm_scale

def cross_spectra(first_spectra, second_spectra, live_mask):
    first_spectra = first_spectra.astype(jnp.float32)
    second_spectra = second_spectra.astype(jnp.float32)
    real_part = jnp.einsum('gkpi,gkpj->kpij', first_spectra[:, 0], second_spectra[:, 0]) + jnp.einsum('gkpi,gkpj->kpij', first_spectra[:, 1], second_spectra[:, 1])
    imag_part = jnp.einsum('gkpi,gkpj->kpij', first_spectra[:, 1], second_spectra[:, 0]) - jnp.einsum('gkpi,gkpj->kpij', first_spectra[:, 0], second_spectra[:, 1])
    stacked = jnp.concatenate([real_part, imag_part], 0) * live_mask[None, :, None, None]
    return stacked.reshape(stacked.shape[0], -1)

def reference(ingest, seg_offsets, pair_blocks, pair_count):
    segments, record_span_duration, stations = ingest.shape
    traces = jax.vmap(lambda buffer_rows, offset: jnp.roll(buffer_rows, -offset, axis=0))(ingest, seg_offsets)
    whitened = whiten(traces)
    twiddles = dft_table(0, record_span_duration, record_span_duration)
    spectra = lax.map(lambda seg_rows: jnp.dot(twiddles, seg_rows, preferred_element_type=jnp.float32).astype(jnp.bfloat16), whitened)
    station_group_matrix = spectra.reshape(segments, 2, record_span_duration, stations // BLOCK_STA, BLOCK_STA)
    first_spectra = jnp.take(station_group_matrix, pair_blocks[0], axis=3)
    second_spectra = jnp.take(station_group_matrix, pair_blocks[1], axis=3)
    slot_index = jnp.arange(PAIR_SLOTS, dtype=jnp.int32)
    live_mask = (slot_index % PAIR_CAP < jnp.take(pair_count, slot_index // PAIR_CAP)).astype(jnp.float32)
    cross_terms = cross_spectra(first_spectra, second_spectra, live_mask)
    lag_rows = lag_offsets_table(0, 2 * MAXLAG, 0, record_span_duration, record_span_duration, segments, MAXLAG)
    return jnp.dot(lag_rows, cross_terms, precision=lax.Precision.HIGHEST, preferred_element_type=jnp.float32)
```

```python
import functools
import math

import jax
import jax.numpy as jnp
import ml_dtypes
import numpy as np
from jax import lax
from jax.experimental import pallas as pl
from jax.experimental.pallas import tpu as pltpu
from jax.sharding import PartitionSpec as P

MAXLAG = 600
BLOCK = 8
HALF_TAPS = 10
FLOOR = 0.5
MESH = pl.DeviceIdType.MESH
F32 = jnp.float32
BF16 = jnp.bfloat16


def dft_tables(samples, bands):
    period = 2 * samples
    t = np.arange(samples)[:, None]
    tables = []
    for band in range(bands):
        k = np.arange(band, samples, bands)[None, :]
        angle = (k * t % period) * (2.0 * math.pi / period)
        tables.append(np.concatenate([np.cos(angle), -np.sin(angle)], 1))
    return np.stack(tables).astype(ml_dtypes.bfloat16)


def lag_tables(samples, bands, segments, groups, pad):
    period = 2 * samples
    per = 2 * MAXLAG // groups
    scale = 1.0 / (period * math.sqrt(samples * segments))
    tables = np.zeros((bands, groups, pad, 2 * samples // bands), np.float64)
    for band in range(bands):
        k = np.arange(band, samples, bands)[None, :]
        weight = np.where(k == 0, 1.0, 2.0) * scale
        tau = (np.arange(2 * MAXLAG) - MAXLAG)[:, None] % period
        angle = (k * tau % period) * (2.0 * math.pi / period)
        rows = np.concatenate([np.cos(angle) * weight, -np.sin(angle) * weight], 1)
        tables[band, :, :per] = rows.reshape(groups, per, -1)
    return tables.astype(ml_dtypes.bfloat16)


def kernel(
    owners, segs, slots, per,
    blocks_ref, count_ref, offset_ref, ingest_ref, dft_hbm, lag_hbm,
    out_ref,
    dft_v, lag_v, ids_v, traces_v, picked_v, white_v, cross_v,
    core_send, core_recv, seg_send, seg_recv,
    table_sem, ids_ssem, ids_rsem, tr_ssem, tr_rsem,
    wh_ssem, wh_rsem, core_ssem, core_rsem, seg_ssem, seg_rsem,
):
    z = lax.axis_index("sta")
    g = lax.axis_index("seg")
    f = lax.axis_index("frq")
    other = 1 - f
    rows, stations = ingest_ref.shape[1:]
    width = slots * BLOCK
    samples = rows * owners
    bins = samples // 2
    pad = lag_v.shape[1]

    dft_copy = pltpu.make_async_copy(dft_hbm.at[f], dft_v, table_sem.at[0])
    lag_copy = pltpu.make_async_copy(lag_hbm.at[f], lag_v, table_sem.at[1])
    dft_copy.start()
    lag_copy.start()

    sub = lax.broadcasted_iota(jnp.int32, (8, 128), 0)
    tile = jnp.zeros((8, 128), jnp.int32)
    for q in range(slots):
        tile = jnp.where(sub == q, blocks_ref[f, q], tile)
    ids_v[0] = tile

    barrier = pltpu.get_barrier_semaphore()
    for d in range(1, owners):
        pl.semaphore_signal(
            barrier, inc=1, device_id={"sta": lax.rem(z + d, owners)}, device_id_type=MESH
        )
    for d in range(1, segs):
        pl.semaphore_signal(
            barrier, inc=1, device_id={"seg": lax.rem(g + d, segs)}, device_id_type=MESH
        )
    pl.semaphore_signal(barrier, inc=1, device_id={"frq": other}, device_id_type=MESH)
    pl.semaphore_wait(barrier, owners + segs - 1)

    ids_copies = []
    for d in range(1, owners):
        copy = pltpu.make_async_remote_copy(
            src_ref=ids_v.at[0],
            dst_ref=ids_v.at[d],
            send_sem=ids_ssem.at[d],
            recv_sem=ids_rsem.at[d],
            device_id={"sta": lax.rem(z + d, owners)},
            device_id_type=MESH,
        )
        copy.start()
        ids_copies.append(copy)

    lane_station = lax.broadcasted_iota(jnp.int32, (8, stations), 1)
    sub_station = lax.broadcasted_iota(jnp.int32, (8, stations), 0)

    def pick(ids):
        hot = []
        for q in range(slots):
            block = jnp.broadcast_to(ids[q : q + 1, 0:1], (8, stations))
            hot.append((block * BLOCK + sub_station == lane_station).astype(F32))
        hot = jnp.concatenate(hot, 0).astype(BF16)
        picked = lax.dot_general(
            hot, ingest_ref[0], (((1,), (1,)), ((), ())), preferred_element_type=F32
        )
        return picked.astype(BF16)

    traces_v[z] = pick(tile)
    trace_copies = []
    for d in range(1, owners):
        ids_copies[d - 1].wait_recv()
        picked_v[d] = pick(ids_v[d])
        copy = pltpu.make_async_remote_copy(
            src_ref=picked_v.at[d],
            dst_ref=traces_v.at[z],
            send_sem=tr_ssem.at[d],
            recv_sem=tr_rsem.at[d],
            device_id={"sta": lax.rem(z + owners - d, owners)},
            device_id_type=MESH,
        )
        copy.start()
        trace_copies.append(copy)
    for copy in trace_copies:
        copy.wait_recv()

    offset = offset_ref[0]
    x = jnp.concatenate([traces_v[s] for s in range(owners)], 1).astype(F32)
    lane = lax.broadcasted_iota(jnp.int32, (width, samples), 1)
    t = lane - offset
    t = jnp.where(t < 0, t + samples, t)
    magnitude = jnp.abs(x)
    zero = jnp.zeros_like(magnitude)
    head = jnp.where(t < samples // 2, magnitude, zero)
    tail = jnp.where(t < samples // 2, zero, magnitude)
    halves = jnp.concatenate([head, tail], 0).astype(BF16)
    halves = jnp.concatenate([halves[:, samples - 128 :], halves, halves[:, :128]], 1)
    near = lax.broadcasted_iota(jnp.int32, (512, 256), 0) - 128
    near = near - lax.broadcasted_iota(jnp.int32, (512, 256), 1)
    band = (jnp.abs(near) <= HALF_TAPS).astype(F32).astype(BF16)
    for j in range(samples // 256):
        cols = slice(256 * j, 256 * j + 256)
        sums = jnp.dot(
            halves[:, 256 * j : 256 * j + 512], band, preferred_element_type=F32
        )
        head_sum, tail_sum = sums[:width], sums[width:]
        tj = t[:, cols]
        level = jnp.where(tj < samples // 4 * 3, head_sum, 0.0)
        level = level + jnp.where(tj >= samples // 4, tail_sum, 0.0)
        level = level / (2 * HALF_TAPS + 1)
        white_v[f, :, cols] = (x[:, cols] / jnp.maximum(level, FLOOR)).astype(BF16)

    white_copy = pltpu.make_async_remote_copy(
        src_ref=white_v.at[f],
        dst_ref=white_v.at[f],
        send_sem=wh_ssem,
        recv_sem=wh_rsem,
        device_id={"frq": other},
        device_id_type=MESH,
    )
    white_copy.start()
    dft_copy.wait()
    white_copy.wait_recv()

    flip = jnp.where((lane < offset) & (f == 1), -1.0, 1.0).astype(BF16)
    both = jnp.concatenate([white_v[0] * flip, white_v[1] * flip], 0)
    live = count_ref[0]
    for m in range(bins // 256):
        re = jnp.dot(both, dft_v[:, 256 * m : 256 * m + 256], preferred_element_type=F32)
        im = jnp.dot(
            both, dft_v[:, bins + 256 * m : bins + 256 * m + 256], preferred_element_type=F32
        )
        for q in range(slots):
            keep = jnp.where(q < live, 1.0, 0.0)
            first = slice(q * BLOCK, q * BLOCK + BLOCK)
            second = slice(width + q * BLOCK, width + q * BLOCK + BLOCK)
            a_re, a_im = re[first] * keep, im[first] * keep
            b_re, b_im = re[second], im[second]
            c_re, c_im = [], []
            for i in range(BLOCK):
                ar = jnp.broadcast_to(a_re[i : i + 1], (BLOCK, 256))
                ai = jnp.broadcast_to(a_im[i : i + 1], (BLOCK, 256))
                c_re.append(ar * b_re + ai * b_im)
                c_im.append(ai * b_re - ar * b_im)
            span = slice(q * BLOCK * BLOCK, (q + 1) * BLOCK * BLOCK)
            cross_v[span, 256 * m : 256 * m + 256] = jnp.concatenate(c_re, 0).astype(BF16)
            cross_v[span, bins + 256 * m : bins + 256 * m + 256] = jnp.concatenate(
                c_im, 0
            ).astype(BF16)

    lag_copy.wait()

    def lag_sums(seg, frq):
        return lax.dot_general(
            lag_v[seg * 2 + frq],
            cross_v[...],
            (((1,), (1,)), ((), ())),
            preferred_element_type=F32,
        )

    core_copies = []
    for j in range(segs):
        d = (j + 1) % segs
        seg = lax.rem(g + d, segs)
        core_send[d] = lag_sums(seg, other).astype(BF16)
        copy = pltpu.make_async_remote_copy(
            src_ref=core_send.at[d],
            dst_ref=core_recv.at[d],
            send_sem=core_ssem.at[d],
            recv_sem=core_rsem.at[d],
            device_id={"frq": other},
            device_id_type=MESH,
        )
        copy.start()
        core_copies.append(copy)
    seg_copies = []
    for d in range(1, segs):
        seg = lax.rem(g + d, segs)
        own = lag_sums(seg, f)
        core_copies[d - 1].wait_recv()
        seg_send[d] = (own + core_recv[d].astype(F32)).astype(BF16)
        copy = pltpu.make_async_remote_copy(
            src_ref=seg_send.at[d],
            dst_ref=seg_recv.at[d],
            send_sem=seg_ssem.at[d],
            recv_sem=seg_rsem.at[d],
            device_id={"seg": seg},
            device_id_type=MESH,
        )
        copy.start()
        seg_copies.append(copy)
    total = lag_sums(g, f)
    core_copies[segs - 1].wait_recv()
    total = total + core_recv[0].astype(F32)
    for d in range(1, segs):
        seg_copies[d - 1].wait_recv()
        total = total + seg_recv[d].astype(F32)
    out_ref[...] = total[:per]

    for copy in ids_copies + trace_copies + [white_copy] + core_copies + seg_copies:
        copy.wait_send()


def on_device(ingest, seg_offsets, pair_blocks, pair_count):
    owners = lax.axis_size("sta")
    segs = lax.axis_size("seg")
    bands = lax.axis_size("frq")
    groups = segs * bands
    _, rows, stations = ingest.shape
    samples = rows * owners
    slots = pair_blocks.shape[1]
    width = slots * BLOCK
    pairs = slots * BLOCK * BLOCK
    per = 2 * MAXLAG // groups
    pad = -(-per // 16) * 16
    dft = jnp.asarray(dft_tables(samples, bands))
    lags = jnp.asarray(lag_tables(samples, bands, segs, groups, pad))
    smem = pl.BlockSpec(memory_space=pltpu.SMEM)
    vmem = pl.BlockSpec(memory_space=pltpu.VMEM)
    hbm = pl.BlockSpec(memory_space=pl.ANY)
    dma = pltpu.SemaphoreType.DMA
    return pl.pallas_call(
        functools.partial(kernel, owners, segs, slots, per),
        out_shape=jax.ShapeDtypeStruct((per, pairs), F32),
        in_specs=[smem, smem, smem, vmem, hbm, hbm],
        out_specs=vmem,
        scratch_shapes=[
            pltpu.VMEM((samples, samples), BF16),
            pltpu.VMEM((groups, pad, samples), BF16),
            pltpu.VMEM((owners, 8, 128), jnp.int32),
            pltpu.VMEM((owners, width, rows), BF16),
            pltpu.VMEM((owners, width, rows), BF16),
            pltpu.VMEM((bands, width, samples), BF16),
            pltpu.VMEM((pairs, samples), BF16),
            pltpu.VMEM((segs, pad, pairs), BF16),
            pltpu.VMEM((segs, pad, pairs), BF16),
            pltpu.VMEM((segs, pad, pairs), BF16),
            pltpu.VMEM((segs, pad, pairs), BF16),
            dma((2,)),
            dma((owners,)),
            dma((owners,)),
            dma((owners,)),
            dma((owners,)),
            dma,
            dma,
            dma((segs,)),
            dma((segs,)),
            dma((segs,)),
            dma((segs,)),
        ],
        compiler_params=pltpu.CompilerParams(
            collective_id=0, has_side_effects=True, vmem_limit_bytes=48 * 1024 * 1024
        ),
    )(pair_blocks, pair_count, seg_offsets, ingest, dft, lags)


def solution(mesh):
    placed = (P(("win", "seg"), "sta", None), P(("win", "seg")), P(None, "sta"), P("sta"))
    return jax.shard_map(
        on_device,
        mesh=mesh,
        in_specs=placed,
        out_specs=P(("seg", "frq"), ("win", "sta")),
        check_vma=False,
    )
```

```python
import functools
import math

import jax
import jax.numpy as jnp
import ml_dtypes
import numpy as np
from jax import lax
from jax.experimental import pallas as pl
from jax.experimental.pallas import tpu as pltpu
from jax.sharding import PartitionSpec as P

MAXLAG = 600
BLOCK = 8
HALF_TAPS = 10
FLOOR = 0.5
MESH = pl.DeviceIdType.MESH
F32 = jnp.float32
BF16 = jnp.bfloat16


def dft_tables(samples, bands):
    period = 2 * samples
    t = np.arange(samples)[:, None]
    tables = []
    for band in range(bands):
        k = np.arange(band, samples, bands)[None, :]
        angle = (k * t % period) * (2.0 * math.pi / period)
        tables.append(np.concatenate([np.cos(angle), -np.sin(angle)], 1))
    return np.stack(tables).astype(ml_dtypes.bfloat16)


def lag_tables(samples, bands, segments, segments_axis, pad):
    groups = segments_axis * bands
    period = 2 * samples
    per = 2 * MAXLAG // groups
    scale = 1.0 / (period * math.sqrt(samples * segments))
    tables = np.zeros((bands, groups, pad, 2 * samples // bands), np.float64)
    for band in range(bands):
        k = np.arange(band, samples, bands)[None, :]
        weight = np.where(k == 0, 1.0, 2.0) * scale
        tau = (np.arange(2 * MAXLAG) - MAXLAG)[:, None] % period
        angle = (k * tau % period) * (2.0 * math.pi / period)
        rows = np.concatenate([np.cos(angle) * weight, -np.sin(angle) * weight], 1)
        tables[band, :, :per] = rows.reshape(groups, per, -1)
    tables = tables.reshape(bands, segments_axis, bands, pad, -1)
    return tables.astype(ml_dtypes.bfloat16)


def kernel(
    owners, segs, slots, per,
    blocks_hbm, count_ref, offset_ref, ingest_hbm, dft_hbm, lag_hbm,
    out_ref,
    blocks_ref, ingest_ref, dft_v, lag_v, ids_v, off_v, traces_v, picked_v, white_v,
    cross_v, core_send, core_recv,
    table_sem, ids_ssem, ids_rsem, off_ssem, off_rsem, tr_ssem, tr_rsem,
    seg_ssem, seg_rsem, wh_ssem, wh_rsem, core_ssem, core_rsem,
):
    z = lax.axis_index("sta")
    g = lax.axis_index("seg")
    f = lax.axis_index("frq")
    other = 1 - f
    rows, stations = ingest_ref.shape[1:]
    width = slots * BLOCK
    samples = rows * owners
    bins = samples // 2

    blocks_copy = pltpu.make_async_copy(blocks_hbm, blocks_ref, table_sem.at[2])
    blocks_copy.start()
    ingest_copy = pltpu.make_async_copy(ingest_hbm, ingest_ref, table_sem.at[3])
    ingest_copy.start()
    dft_copy = pltpu.make_async_copy(dft_hbm.at[f], dft_v, table_sem.at[0])
    lag_copy = pltpu.make_async_copy(lag_hbm.at[f, g], lag_v, table_sem.at[1])
    dft_copy.start()
    lag_copy.start()

    barrier = pltpu.get_barrier_semaphore()
    for d in range(1, owners):
        pl.semaphore_signal(
            barrier, inc=1, device_id={"sta": lax.rem(z + d, owners)}, device_id_type=MESH
        )
    for d in range(1, segs):
        pl.semaphore_signal(
            barrier, inc=1, device_id={"seg": lax.rem(g + d, segs)}, device_id_type=MESH
        )
    pl.semaphore_signal(barrier, inc=1, device_id={"frq": other}, device_id_type=MESH)
    pl.semaphore_wait(barrier, owners + segs - 1)

    blocks_copy.wait()
    sub = lax.broadcasted_iota(jnp.int32, (8, 128), 0)
    tile = jnp.zeros((8, 128), jnp.int32)
    for q in range(slots):
        tile = jnp.where(sub == q, blocks_ref[f, q], tile)
    ids_v[0] = tile

    ids_copies = []
    for d in range(1, owners):
        copy = pltpu.make_async_remote_copy(
            src_ref=ids_v.at[0],
            dst_ref=ids_v.at[d],
            send_sem=ids_ssem.at[d],
            recv_sem=ids_rsem.at[d],
            device_id={"sta": lax.rem(z + d, owners)},
            device_id_type=MESH,
        )
        copy.start()
        ids_copies.append(copy)

    off_v[0] = jnp.full((8, 128), offset_ref[0], jnp.int32)
    off_copies = []
    for d in range(1, segs):
        copy = pltpu.make_async_remote_copy(
            src_ref=off_v.at[0],
            dst_ref=off_v.at[d],
            send_sem=off_ssem.at[d],
            recv_sem=off_rsem.at[d],
            device_id={"seg": lax.rem(g + d, segs)},
            device_id_type=MESH,
        )
        copy.start()
        off_copies.append(copy)

    lane_station = lax.broadcasted_iota(jnp.int32, (8, stations), 1)
    sub_station = lax.broadcasted_iota(jnp.int32, (8, stations), 0)

    def pick(ids):
        hot = []
        for q in range(slots):
            block = jnp.broadcast_to(ids[q : q + 1, 0:1], (8, stations))
            hot.append((block * BLOCK + sub_station == lane_station).astype(F32))
        hot = jnp.concatenate(hot, 0).astype(BF16)
        picked = lax.dot_general(
            hot, ingest_ref[0], (((1,), (1,)), ((), ())), preferred_element_type=F32
        )
        return picked.astype(BF16)

    seg_copies = [[] for _ in range(segs)]

    def pass_on(k):
        source = lax.rem(z + k, owners)
        for d in range(1, segs):
            copy = pltpu.make_async_remote_copy(
                src_ref=traces_v.at[0, source],
                dst_ref=traces_v.at[d, source],
                send_sem=seg_ssem.at[d, k],
                recv_sem=seg_rsem.at[d, k],
                device_id={"seg": lax.rem(g + d, segs)},
                device_id_type=MESH,
            )
            copy.start()
            seg_copies[d].append(copy)

    ingest_copy.wait()
    traces_v[0, z] = pick(tile)
    pass_on(0)
    trace_copies = []
    for d in range(1, owners):
        ids_copies[d - 1].wait_recv()
        picked_v[d] = pick(ids_v[d])
        copy = pltpu.make_async_remote_copy(
            src_ref=picked_v.at[d],
            dst_ref=traces_v.at[0, z],
            send_sem=tr_ssem.at[d],
            recv_sem=tr_rsem.at[d],
            device_id={"sta": lax.rem(z + owners - d, owners)},
            device_id_type=MESH,
        )
        copy.start()
        trace_copies.append(copy)
    for k in range(1, owners):
        trace_copies[k - 1].wait_recv()
        pass_on(k)

    near = lax.broadcasted_iota(jnp.int32, (512, 256), 0) - 128
    near = near - lax.broadcasted_iota(jnp.int32, (512, 256), 1)
    band = (jnp.abs(near) <= HALF_TAPS).astype(F32).astype(BF16)
    lane = lax.broadcasted_iota(jnp.int32, (1, samples), 1)

    def offset_row(d):
        return jnp.broadcast_to(off_v[d][0:1, 0:1], (1, samples))

    def whiten(d):
        x = jnp.concatenate([traces_v[d, s] for s in range(owners)], 1).astype(F32)
        t = lane - offset_row(d)
        t = jnp.where(t < 0, t + samples, t)
        magnitude = jnp.abs(x)
        is_head = (t < samples // 2).astype(F32)
        head = magnitude * is_head
        tail = magnitude - head
        halves = jnp.concatenate([head, tail], 0).astype(BF16)
        halves = jnp.concatenate([halves[:, samples - 128 :], halves, halves[:, :128]], 1)
        use_head = (t < samples // 4 * 3).astype(F32)
        use_tail = (t >= samples // 4).astype(F32)
        for j in range(samples // 256):
            cols = slice(256 * j, 256 * j + 256)
            sums = jnp.dot(
                halves[:, 256 * j : 256 * j + 512], band, preferred_element_type=F32
            )
            level = sums[:width] * use_head[:, cols] + sums[width:] * use_tail[:, cols]
            level = level / (2 * HALF_TAPS + 1)
            white_v[d, f, :, cols] = (x[:, cols] / jnp.maximum(level, FLOOR)).astype(BF16)

    white_copies = []
    for d in range(segs):
        if d:
            off_copies[d - 1].wait_recv()
            for copy in seg_copies[d]:
                copy.wait_recv()
        whiten(d)
        copy = pltpu.make_async_remote_copy(
            src_ref=white_v.at[d, f],
            dst_ref=white_v.at[d, f],
            send_sem=wh_ssem.at[d],
            recv_sem=wh_rsem.at[d],
            device_id={"frq": other},
            device_id_type=MESH,
        )
        copy.start()
        white_copies.append(copy)
    dft_copy.wait()

    both = []
    for d in range(segs):
        white_copies[d].wait_recv()
        flip = jnp.where((lane < offset_row(d)) & (f == 1), -1.0, 1.0)
        flip = jnp.broadcast_to(flip, (width, samples)).astype(BF16)
        both += [white_v[d, 0] * flip, white_v[d, 1] * flip]
    both = jnp.concatenate(both, 0)
    live = count_ref[0]
    for m in range(bins // 256):
        re = jnp.dot(both, dft_v[:, 256 * m : 256 * m + 256], preferred_element_type=F32)
        im = jnp.dot(
            both, dft_v[:, bins + 256 * m : bins + 256 * m + 256], preferred_element_type=F32
        )
        for q in range(slots):
            keep = jnp.where(q < live, 1.0, 0.0)
            c_re, c_im = [0.0] * BLOCK, [0.0] * BLOCK
            for d in range(segs):
                first = slice((2 * d * slots + q) * BLOCK, (2 * d * slots + q + 1) * BLOCK)
                second = slice(first.start + width, first.stop + width)
                a_re, a_im = re[first] * keep, im[first] * keep
                b_re, b_im = re[second], im[second]
                for i in range(BLOCK):
                    ar = jnp.broadcast_to(a_re[i : i + 1], (BLOCK, 256))
                    ai = jnp.broadcast_to(a_im[i : i + 1], (BLOCK, 256))
                    c_re[i] = c_re[i] + (ar * b_re + ai * b_im)
                    c_im[i] = c_im[i] + (ai * b_re - ar * b_im)
            span = slice(q * BLOCK * BLOCK, (q + 1) * BLOCK * BLOCK)
            cross_v[span, 256 * m : 256 * m + 256] = jnp.concatenate(c_re, 0).astype(BF16)
            cross_v[span, bins + 256 * m : bins + 256 * m + 256] = jnp.concatenate(
                c_im, 0
            ).astype(BF16)

    lag_copy.wait()

    def lag_sums(frq):
        return lax.dot_general(
            lag_v[frq], cross_v[...], (((1,), (1,)), ((), ())), preferred_element_type=F32
        )

    core_send[...] = lag_sums(other).astype(BF16)
    core_copy = pltpu.make_async_remote_copy(
        src_ref=core_send,
        dst_ref=core_recv,
        send_sem=core_ssem,
        recv_sem=core_rsem,
        device_id={"frq": other},
        device_id_type=MESH,
    )
    core_copy.start()
    total = lag_sums(f)
    core_copy.wait_recv()
    out_ref[...] = (total + core_recv[...].astype(F32))[:per]

    for copy in ids_copies + off_copies + trace_copies + sum(seg_copies, []):
        copy.wait_send()
    for copy in white_copies + [core_copy]:
        copy.wait_send()


def on_device(ingest, seg_offsets, pair_blocks, pair_count):
    owners = lax.axis_size("sta")
    segs = lax.axis_size("seg")
    bands = lax.axis_size("frq")
    groups = segs * bands
    _, rows, stations = ingest.shape
    samples = rows * owners
    slots = pair_blocks.shape[1]
    width = slots * BLOCK
    pairs = slots * BLOCK * BLOCK
    per = 2 * MAXLAG // groups
    pad = -(-per // 16) * 16
    dft = jnp.asarray(dft_tables(samples, bands))
    lags = jnp.asarray(lag_tables(samples, bands, segs, segs, pad))
    smem = pl.BlockSpec(memory_space=pltpu.SMEM)
    vmem = pl.BlockSpec(memory_space=pltpu.VMEM)
    hbm = pl.BlockSpec(memory_space=pl.ANY)
    dma = pltpu.SemaphoreType.DMA
    return pl.pallas_call(
        functools.partial(kernel, owners, segs, slots, per),
        out_shape=jax.ShapeDtypeStruct((per, pairs), F32),
        in_specs=[hbm, smem, smem, hbm, hbm, hbm],
        out_specs=vmem,
        scratch_shapes=[
            pltpu.SMEM(pair_blocks.shape, jnp.int32),
            pltpu.VMEM(ingest.shape, BF16),
            pltpu.VMEM((samples, samples), BF16),
            pltpu.VMEM((bands, pad, samples), BF16),
            pltpu.VMEM((owners, 8, 128), jnp.int32),
            pltpu.VMEM((segs, 8, 128), jnp.int32),
            pltpu.VMEM((segs, owners, width, rows), BF16),
            pltpu.VMEM((owners, width, rows), BF16),
            pltpu.VMEM((segs, bands, width, samples), BF16),
            pltpu.VMEM((pairs, samples), BF16),
            pltpu.VMEM((pad, pairs), BF16),
            pltpu.VMEM((pad, pairs), BF16),
            dma((4,)),
            dma((owners,)),
            dma((owners,)),
            dma((segs,)),
            dma((segs,)),
            dma((owners,)),
            dma((owners,)),
            dma((segs, owners)),
            dma((segs, owners)),
            dma((segs,)),
            dma((segs,)),
            dma,
            dma,
        ],
        compiler_params=pltpu.CompilerParams(
            collective_id=0, has_side_effects=True, vmem_limit_bytes=58 * 1024 * 1024
        ),
    )(pair_blocks, pair_count, seg_offsets, ingest, dft, lags)


def solution(mesh):
    placed = (P(("win", "seg"), "sta", None), P(("win", "seg")), P(None, "sta"), P("sta"))
    return jax.shard_map(
        on_device,
        mesh=mesh,
        in_specs=placed,
        out_specs=P(("seg", "frq"), ("win", "sta")),
        check_vma=False,
    )
```

```python
import functools
import math

import jax
import jax.numpy as jnp
import ml_dtypes
import numpy as np
from jax import lax
from jax.experimental import pallas as pl
from jax.experimental.pallas import tpu as pltpu
from jax.sharding import PartitionSpec as P

MAXLAG = 600
BLOCK = 8
CHUNK = 16
HALF_TAPS = 10
FLOOR = 0.5
MESH = pl.DeviceIdType.MESH
F32 = jnp.float32
BF16 = jnp.bfloat16


def dft_tables(samples, bands):
    period = 2 * samples
    t = np.arange(samples)[:, None]
    tables = []
    for band in range(bands):
        k = np.arange(band, samples, bands)[None, :]
        angle = (k * t % period) * (2.0 * math.pi / period)
        tables.append(np.concatenate([np.cos(angle), -np.sin(angle)], 1))
    return np.stack(tables).astype(ml_dtypes.bfloat16)


def lag_tables(samples, bands, segments, segments_axis, pad):
    groups = segments_axis * bands
    period = 2 * samples
    per = 2 * MAXLAG // groups
    scale = 1.0 / (period * math.sqrt(samples * segments))
    tables = np.zeros((bands, groups, pad, 2 * samples // bands), np.float64)
    for band in range(bands):
        k = np.arange(band, samples, bands)[None, :]
        weight = np.where(k == 0, 1.0, 2.0) * scale
        tau = (np.arange(2 * MAXLAG) - MAXLAG)[:, None] % period
        angle = (k * tau % period) * (2.0 * math.pi / period)
        rows = np.concatenate([np.cos(angle) * weight, -np.sin(angle) * weight], 1)
        tables[band, :, :per] = rows.reshape(groups, per, -1)
    tables = tables.reshape(bands, segments_axis, bands, pad, -1)
    return tables.astype(ml_dtypes.bfloat16)


def kernel(
    owners, segs, slots, per,
    blocks_hbm, count_ref, offset_ref, ingest_hbm, dft_hbm, lag_hbm,
    out_ref,
    blocks_ref, ingest_ref, dft_v, lag_v, ids_v, off_v, traces_v, picked_v, white_v,
    cross_v, core_send, core_recv,
    table_sem, ids_ssem, ids_rsem, off_ssem, off_rsem, tr_ssem, tr_rsem,
    seg_ssem, seg_rsem, wh_ssem, wh_rsem, core_ssem, core_rsem,
):
    z = lax.axis_index("sta")
    g = lax.axis_index("seg")
    f = lax.axis_index("frq")
    other = 1 - f
    rows, stations = ingest_ref.shape[1:]
    width = slots * BLOCK
    samples = rows * owners
    bins = samples // 2

    blocks_copy = pltpu.make_async_copy(blocks_hbm, blocks_ref, table_sem.at[2])
    blocks_copy.start()
    ingest_copy = pltpu.make_async_copy(ingest_hbm, ingest_ref, table_sem.at[3])
    ingest_copy.start()
    dft_copy = pltpu.make_async_copy(dft_hbm.at[f], dft_v, table_sem.at[0])
    lag_copy = pltpu.make_async_copy(lag_hbm.at[f, g], lag_v, table_sem.at[1])
    dft_copy.start()
    lag_copy.start()

    barrier = pltpu.get_barrier_semaphore()
    for d in range(1, owners):
        pl.semaphore_signal(
            barrier, inc=1, device_id={"sta": lax.rem(z + d, owners)}, device_id_type=MESH
        )
    for d in range(1, segs):
        pl.semaphore_signal(
            barrier, inc=1, device_id={"seg": lax.rem(g + d, segs)}, device_id_type=MESH
        )
    pl.semaphore_signal(barrier, inc=1, device_id={"frq": other}, device_id_type=MESH)
    pl.semaphore_wait(barrier, owners + segs - 1)

    blocks_copy.wait()
    sub = lax.broadcasted_iota(jnp.int32, (8, 128), 0)
    tile = jnp.zeros((8, 128), jnp.int32)
    for q in range(slots):
        tile = jnp.where(sub == q, blocks_ref[f, q], tile)
    ids_v[0] = tile

    way = jnp.where(z < owners // 2, 1, owners - 1)
    step = [lax.rem(way * j, owners) for j in range(owners)]
    ids_copies = []
    for j in range(owners - 1, 0, -1):
        d = step[j]
        copy = pltpu.make_async_remote_copy(
            src_ref=ids_v.at[0],
            dst_ref=ids_v.at[d],
            send_sem=ids_ssem.at[d],
            recv_sem=ids_rsem.at[d],
            device_id={"sta": lax.rem(z + d, owners)},
            device_id_type=MESH,
        )
        copy.start()
        ids_copies.append(copy)

    off_v[0] = jnp.full((8, 128), offset_ref[0], jnp.int32)
    off_copies = []
    for d in range(1, segs):
        copy = pltpu.make_async_remote_copy(
            src_ref=off_v.at[0],
            dst_ref=off_v.at[d],
            send_sem=off_ssem.at[d],
            recv_sem=off_rsem.at[d],
            device_id={"seg": lax.rem(g + d, segs)},
            device_id_type=MESH,
        )
        copy.start()
        off_copies.append(copy)

    lane_station = lax.broadcasted_iota(jnp.int32, (8, stations), 1)
    sub_station = lax.broadcasted_iota(jnp.int32, (8, stations), 0)

    def pick(ids):
        hot = []
        for q in range(slots):
            block = jnp.broadcast_to(ids[q : q + 1, 0:1], (8, stations))
            hot.append((block * BLOCK + sub_station == lane_station).astype(F32))
        hot = jnp.concatenate(hot, 0).astype(BF16)
        picked = lax.dot_general(
            hot, ingest_ref[0], (((1,), (1,)), ((), ())), preferred_element_type=F32
        )
        return picked.astype(BF16)

    parts = [pl.ds(CHUNK * c, CHUNK) for c in range(width // CHUNK)]
    seg_copies = [[[] for _ in parts] for _ in range(segs)]

    def pass_on(k, c):
        source = lax.rem(z + k, owners)
        for d in range(1, segs):
            copy = pltpu.make_async_remote_copy(
                src_ref=traces_v.at[0, source, parts[c]],
                dst_ref=traces_v.at[d, source, parts[c]],
                send_sem=seg_ssem.at[d, k, c],
                recv_sem=seg_rsem.at[d, k, c],
                device_id={"seg": lax.rem(g + d, segs)},
                device_id_type=MESH,
            )
            copy.start()
            seg_copies[d][c].append(copy)

    trace_copies = [[] for _ in parts]

    def send_picked(d, c):
        copy = pltpu.make_async_remote_copy(
            src_ref=picked_v.at[d, parts[c]],
            dst_ref=traces_v.at[0, z, parts[c]],
            send_sem=tr_ssem.at[d, c],
            recv_sem=tr_rsem.at[d, c],
            device_id={"sta": lax.rem(z + owners - d, owners)},
            device_id_type=MESH,
        )
        copy.start()
        trace_copies[c].append(copy)

    ingest_copy.wait()
    traces_v[0, z] = pick(tile)
    for c in range(len(parts)):
        pass_on(0, c)
    for j in range(1, owners):
        ids_copies[j - 1].wait_recv()
        d = step[owners - j]
        picked_v[d] = pick(ids_v[d])
        send_picked(d, 0)
    for c in range(1, len(parts)):
        for j in range(1, owners):
            send_picked(step[owners - j], c)
    for c in range(len(parts)):
        for j in range(1, owners):
            trace_copies[c][owners - j - 1].wait_recv()
            pass_on(step[j], c)

    near = lax.broadcasted_iota(jnp.int32, (512, 256), 0) - 128
    near = near - lax.broadcasted_iota(jnp.int32, (512, 256), 1)
    band = (jnp.abs(near) <= HALF_TAPS).astype(F32).astype(BF16)
    lane = lax.broadcasted_iota(jnp.int32, (1, samples), 1)

    def offset_row(d):
        return jnp.broadcast_to(off_v[d][0:1, 0:1], (1, samples))

    def whiten(d, first, count):
        span = slice(first, first + count)
        x = jnp.concatenate([traces_v[d, s, span] for s in range(owners)], 1).astype(F32)
        t = lane - offset_row(d)
        t = jnp.where(t < 0, t + samples, t)
        magnitude = jnp.abs(x)
        is_head = (t < samples // 2).astype(F32)
        head = magnitude * is_head
        tail = magnitude - head
        halves = jnp.concatenate([head, tail], 0).astype(BF16)
        halves = jnp.concatenate([halves[:, samples - 128 :], halves, halves[:, :128]], 1)
        use_head = (t < samples // 4 * 3).astype(F32)
        use_tail = (t >= samples // 4).astype(F32)
        stacked = jnp.concatenate(
            [halves[:, 256 * j : 256 * j + 512] for j in range(samples // 256)], 0
        )
        sums = jnp.dot(stacked, band, preferred_element_type=F32)
        for j in range(samples // 256):
            cols = slice(256 * j, 256 * j + 256)
            head_sum = sums[2 * j * count : (2 * j + 1) * count]
            tail_sum = sums[(2 * j + 1) * count : (2 * j + 2) * count]
            level = head_sum * use_head[:, cols] + tail_sum * use_tail[:, cols]
            level = level / (2 * HALF_TAPS + 1)
            white_v[d, f, span, cols] = (x[:, cols] / jnp.maximum(level, FLOOR)).astype(BF16)

    white_copies = [[] for _ in range(segs)]

    def swap_white(d, c, first, count):
        copy = pltpu.make_async_remote_copy(
            src_ref=white_v.at[d, f, pl.ds(first, count)],
            dst_ref=white_v.at[d, f, pl.ds(first, count)],
            send_sem=wh_ssem.at[d, c],
            recv_sem=wh_rsem.at[d, c],
            device_id={"frq": other},
            device_id_type=MESH,
        )
        copy.start()
        white_copies[d].append(copy)

    whiten(0, 0, width)
    swap_white(0, 0, 0, width)
    for d in range(1, segs):
        off_copies[d - 1].wait_recv()
        for c in range(len(parts)):
            for copy in seg_copies[d][c]:
                copy.wait_recv()
            whiten(d, CHUNK * c, CHUNK)
            swap_white(d, c, CHUNK * c, CHUNK)
    dft_copy.wait()

    both = []
    for d in range(segs):
        for copy in white_copies[d]:
            copy.wait_recv()
        flip = jnp.where((lane < offset_row(d)) & (f == 1), -1.0, 1.0)
        flip = jnp.broadcast_to(flip, (width, samples)).astype(BF16)
        both += [white_v[d, 0] * flip, white_v[d, 1] * flip]
    both = jnp.concatenate(both, 0)
    live = count_ref[0]
    for m in range(bins // 256):
        re = jnp.dot(both, dft_v[:, 256 * m : 256 * m + 256], preferred_element_type=F32)
        im = jnp.dot(
            both, dft_v[:, bins + 256 * m : bins + 256 * m + 256], preferred_element_type=F32
        )
        for q in range(slots):
            keep = jnp.where(q < live, 1.0, 0.0)
            c_re, c_im = [0.0] * BLOCK, [0.0] * BLOCK
            for d in range(segs):
                first = slice((2 * d * slots + q) * BLOCK, (2 * d * slots + q + 1) * BLOCK)
                second = slice(first.start + width, first.stop + width)
                a_re, a_im = re[first] * keep, im[first] * keep
                b_re, b_im = re[second], im[second]
                for i in range(BLOCK):
                    ar = jnp.broadcast_to(a_re[i : i + 1], (BLOCK, 256))
                    ai = jnp.broadcast_to(a_im[i : i + 1], (BLOCK, 256))
                    c_re[i] = c_re[i] + (ar * b_re + ai * b_im)
                    c_im[i] = c_im[i] + (ai * b_re - ar * b_im)
            span = slice(q * BLOCK * BLOCK, (q + 1) * BLOCK * BLOCK)
            cross_v[span, 256 * m : 256 * m + 256] = jnp.concatenate(c_re, 0).astype(BF16)
            cross_v[span, bins + 256 * m : bins + 256 * m + 256] = jnp.concatenate(
                c_im, 0
            ).astype(BF16)

    lag_copy.wait()

    def lag_sums(frq, first, count):
        return lax.dot_general(
            lag_v[frq, first : first + count],
            cross_v[...],
            (((1,), (1,)), ((), ())),
            preferred_element_type=F32,
        )

    pad = lag_v.shape[1]
    cut = (pad // 2 + 15) // 16 * 16
    core_copies = []
    for h, (first, count) in enumerate([(0, cut), (cut, pad - cut)]):
        core_send[first : first + count] = lag_sums(other, first, count).astype(BF16)
        copy = pltpu.make_async_remote_copy(
            src_ref=core_send.at[pl.ds(first, count)],
            dst_ref=core_recv.at[pl.ds(first, count)],
            send_sem=core_ssem.at[h],
            recv_sem=core_rsem.at[h],
            device_id={"frq": other},
            device_id_type=MESH,
        )
        copy.start()
        core_copies.append(copy)
    total = lag_sums(f, 0, pad)
    core_copies[0].wait_recv()
    out_ref[:cut] = total[:cut] + core_recv[:cut].astype(F32)
    core_copies[1].wait_recv()
    out_ref[cut:] = (total[cut:] + core_recv[cut:].astype(F32))[: per - cut]

    started = ids_copies + off_copies + core_copies
    started += sum(trace_copies, []) + sum(white_copies, [])
    for by_part in seg_copies:
        started += sum(by_part, [])
    for copy in started:
        copy.wait_send()


def on_device(ingest, seg_offsets, pair_blocks, pair_count):
    owners = lax.axis_size("sta")
    segs = lax.axis_size("seg")
    bands = lax.axis_size("frq")
    groups = segs * bands
    _, rows, stations = ingest.shape
    samples = rows * owners
    slots = pair_blocks.shape[1]
    width = slots * BLOCK
    chunks = width // CHUNK
    pairs = slots * BLOCK * BLOCK
    per = 2 * MAXLAG // groups
    pad = -(-per // 16) * 16
    dft = jnp.asarray(dft_tables(samples, bands))
    lags = jnp.asarray(lag_tables(samples, bands, segs, segs, pad))
    smem = pl.BlockSpec(memory_space=pltpu.SMEM)
    vmem = pl.BlockSpec(memory_space=pltpu.VMEM)
    hbm = pl.BlockSpec(memory_space=pl.ANY)
    dma = pltpu.SemaphoreType.DMA
    return pl.pallas_call(
        functools.partial(kernel, owners, segs, slots, per),
        out_shape=jax.ShapeDtypeStruct((per, pairs), F32),
        in_specs=[hbm, smem, smem, hbm, hbm, hbm],
        out_specs=vmem,
        scratch_shapes=[
            pltpu.SMEM(pair_blocks.shape, jnp.int32),
            pltpu.VMEM(ingest.shape, BF16),
            pltpu.VMEM((samples, samples), BF16),
            pltpu.VMEM((bands, pad, samples), BF16),
            pltpu.VMEM((owners, 8, 128), jnp.int32),
            pltpu.VMEM((segs, 8, 128), jnp.int32),
            pltpu.VMEM((segs, owners, width, rows), BF16),
            pltpu.VMEM((owners, width, rows), BF16),
            pltpu.VMEM((segs, bands, width, samples), BF16),
            pltpu.VMEM((pairs, samples), BF16),
            pltpu.VMEM((pad, pairs), BF16),
            pltpu.VMEM((pad, pairs), BF16),
            dma((4,)),
            dma((owners,)),
            dma((owners,)),
            dma((segs,)),
            dma((segs,)),
            dma((owners, chunks)),
            dma((owners, chunks)),
            dma((segs, owners, chunks)),
            dma((segs, owners, chunks)),
            dma((segs, chunks)),
            dma((segs, chunks)),
            dma((2,)),
            dma((2,)),
        ],
        compiler_params=pltpu.CompilerParams(
            collective_id=0, has_side_effects=True, vmem_limit_bytes=58 * 1024 * 1024
        ),
    )(pair_blocks, pair_count, seg_offsets, ingest, dft, lags)


def solution(mesh):
    placed = (P(("win", "seg"), "sta", None), P(("win", "seg")), P(None, "sta"), P("sta"))
    return jax.shard_map(
        on_device,
        mesh=mesh,
        in_specs=placed,
        out_specs=P(("seg", "frq"), ("win", "sta")),
        check_vma=False,
    )
```
